128 devices in a mesh: owner: 32 (over x, y, core), rep: 4 (over z).
Axes of the slice: x: 4, y: 4, z: 4, core: 2. Of those that a mesh axis runs over, the one named last changes fastest.
Arguments:
- embeddings: bfloat16 [32768, 1024], P(('owner', 'rep')), may hold values from -16 to 16
- cluster: int32 [32768], P(('owner', 'rep')), may hold values from 0 to 15, as said below
Outputs:
- best: float32 [32768], P(('owner', 'rep'))
The draws below stay inside these ranges and needn't reach their ends.
Inputs may be any that keep to these rules, and one draw needn't show every extreme that they name: `cluster`: the clusters c with the same c // 4 form a group. Among the rows of one device at most 128 lie in one group; in every draw one group holds exactly 128 rows of every device.
All inputs are finite; a program needn't handle non-finite values.
Results may differ from the reference program's by a relative error of at most 0.00062.
Values may be sent and summed in bfloat16 or wider, within the bound.
A program may use at most 128 MiB of HBM per device.

```python
import math
import jax
import jax.numpy as jnp
from jax import lax

D = 1024
ROWS_DEV = 256
CL_GRP = 4
PROTO = 4
CLUSTERS = 16
N_OWNER = 32
N_REP = 4


def routing_rows(key):
    key = jax.random.fold_in(key, 11)
    capacity = 2 * ROWS_DEV // N_REP
    slots = N_REP * capacity
    blocks = N_OWNER * N_REP
    total = ROWS_DEV * blocks
    k_star, k_blocks, k_first, k_second = jax.random.split(key, 4)
    forced = jax.random.randint(k_star, (), 0, N_REP)

    def one_block(block_key):
        k_pick, k_order = jax.random.split(block_key)
        picks = jax.random.permutation(k_pick, slots - capacity)[:ROWS_DEV - capacity]
        others = jnp.where(picks >= forced * capacity, picks + capacity, picks)
        chosen = jnp.concatenate([forced * capacity + jnp.arange(capacity), others])
        chosen = jax.random.permutation(k_order, chosen)
        return chosen // capacity
    groups = jax.vmap(one_block)(jax.random.split(k_blocks, blocks)).reshape(total)
    first = jax.random.randint(k_first, (total,), 0, CL_GRP)
    second = jax.random.randint(k_second, (total,), 0, CL_GRP)
    local = first * second // CL_GRP
    return (groups * CL_GRP + local).astype(jnp.int32)


def draw_cluster(key, part):
    return routing_rows(key)


def draw_embeddings(key, part):
    clusters = routing_rows(key)
    key = jax.random.fold_in(key, 5)
    total = ROWS_DEV * N_OWNER * N_REP
    k_proto, k_which, k_noise, k_level = jax.random.split(key, 4)
    protos = jax.random.normal(k_proto, (CLUSTERS * PROTO, D), jnp.float32)
    which = jax.random.randint(k_which, (total,), 0, PROTO)
    family = protos[clusters * PROTO + which]
    noise = jax.random.normal(k_noise, (total, D), jnp.float32)
    level = jnp.exp(jax.random.uniform(k_level, (total,), jnp.float32, math.log(0.3), math.log(3.0)))
    raw = noise + level[:, None] * family
    return jnp.clip(raw, -16.0, 16.0).astype(jnp.bfloat16)


def setup_inputs(seed: int = 0) -> dict:
    keys = jax.random.split(jax.random.key(seed), 3)
    return {
        "embeddings": draw_embeddings(jax.random.fold_in(keys[2], 71), 0),
        "cluster": draw_cluster(jax.random.fold_in(keys[2], 71), 0),
    }


def reference(embeddings, cluster):
    values = embeddings.astype(jnp.float32)
    unit = (values * lax.rsqrt(lax.optimization_barrier(jnp.mean(values * values, axis=-1, keepdims=True)) + 1e-06) * D ** (-0.5)).astype(jnp.bfloat16)
    whole = unit.astype(jnp.float32)
    total = whole.shape[0]
    block = math.gcd(total, 1024)
    row_ids = jnp.arange(total, dtype=jnp.int32)

    def one_block(start):
        rows = lax.dynamic_slice_in_dim(whole, start, block, 0)
        near = lax.dynamic_slice_in_dim(cluster, start, block, 0)
        ids = start + jnp.arange(block, dtype=jnp.int32)
        scores = jnp.dot(rows, whole.T, precision=lax.Precision.HIGHEST)
        same = (near[:, None] == cluster[None, :]) & (ids[:, None] != row_ids[None, :])
        return lax.optimization_barrier(jnp.max(jnp.where(same, scores, jnp.float32(-1.0)), axis=1))
    starts = (jnp.arange(total // block, dtype=jnp.int32) * block).astype(jnp.int32)
    return lax.map(one_block, starts).reshape(total)
```

```python
import jax
import jax.numpy as jnp
from jax import lax
from jax.experimental import pallas as pl
from jax.experimental.pallas import tpu as pltpu
from jax.sharding import PartitionSpec as P

MESH = pl.DeviceIdType.MESH
SIDE = 4
STEPS = ((1, 0, 0), (-1, 0, 0), (0, 1, 0), (0, -1, 0), (0, 0, 1), (0, 0, -1))
CHUNKS = 4
SPOTS = (
    (0, 0, 0),
    (0, 1, 0),
    (0, 3, 0),
    (1, 0, 0),
    (3, 0, 0),
    (1, 0, 1),
    (1, 3, 0),
    (0, 1, 3),
    (1, 1, 1),
    (0, 1, 2),
    (3, 1, 3),
    (2, 3, 0),
)
LEFT = (0, 1, 2, 3, 4, 5, 6, 7, 8, 9)
PARENT = (
    (
        (-1, 0, 0, 0, 0, 3, 2, 1, 5, 7, 7, 6),
        (-1, 0, 0, 0, 0, 3, 3, 1, 5, 7, 7, 6),
        (-1, 0, 0, 0, 0, 3, 2, 1, 5, 7, 7, 6),
        (-1, 0, 0, 0, 0, 3, 3, 1, 5, 7, 7, 6),
    ),
    (
        (-1, 0, 0, 0, 0, 3, 2, 1, 5, 7, 7, 6),
        (-1, 0, 0, 0, 0, 3, 3, 1, 5, 7, 7, 6),
        (-1, 0, 0, 0, 0, 3, 3, 1, 5, 7, 7, 6),
        (-1, 0, 0, 0, 0, 3, 3, 1, 5, 7, 7, 6),
    ),
)
WAY = (
    (
        (-1, 2, 3, 0, 1, 4, 0, 5, 2, 5, 1, 0),
        (-1, 2, 3, 0, 1, 4, 3, 5, 2, 5, 1, 0),
        (-1, 2, 3, 0, 1, 4, 0, 5, 2, 5, 1, 0),
        (-1, 2, 3, 0, 1, 4, 3, 5, 2, 5, 1, 0),
    ),
    (
        (-1, 2, 3, 0, 1, 4, 0, 5, 2, 5, 1, 0),
        (-1, 2, 3, 0, 1, 4, 3, 5, 2, 5, 1, 0),
        (-1, 2, 3, 0, 1, 4, 3, 5, 2, 5, 1, 0),
        (-1, 2, 3, 0, 1, 4, 3, 5, 2, 5, 1, 0),
    ),
)
ORDER = (
    (
        (1, 2, 3, 5, 6, 7, 4, 8, 9, 10, 11),
        (1, 3, 5, 6, 7, 2, 4, 8, 9, 10, 11),
        (1, 2, 3, 5, 6, 7, 4, 8, 9, 10, 11),
        (1, 3, 5, 6, 7, 2, 4, 8, 9, 10, 11),
    ),
    (
        (1, 2, 3, 5, 6, 7, 4, 8, 9, 10, 11),
        (1, 3, 5, 6, 7, 2, 4, 8, 9, 10, 11),
        (1, 3, 5, 6, 7, 2, 4, 8, 9, 10, 11),
        (1, 3, 5, 6, 7, 2, 4, 8, 9, 10, 11),
    ),
)
TASKS = (
    (2, 0), (3, 0, 0), (4, 0), (0, 1, 0), (0, 2, 0), (0, 3, 0), (0, 4, 0), (0, 1, 1), (0, 2, 1), (0, 3, 1),
    (0, 4, 1), (0, 5, 0), (0, 7, 0), (0, 1, 2), (0, 2, 2), (0, 3, 2), (0, 4, 2), (0, 5, 1), (0, 7, 1),
    (0, 1, 3), (1, 1), (0, 2, 3), (1, 2), (0, 3, 3), (1, 3), (0, 4, 3), (1, 4), (0, 9, 0), (2, 1), (3, 0, 1),
    (4, 1), (0, 5, 2), (2, 2), (3, 1, 2), (4, 2), (2, 3), (3, 0, 3), (3, 1, 3), (0, 6, 0), (0, 6, 1),
    (0, 8, 0), (0, 10, 0), (3, 2, 3), (4, 3), (0, 5, 3), (1, 5), (0, 7, 2), (2, 4), (3, 3, 4), (4, 4),
    (0, 6, 2), (2, 5), (3, 0, 5), (0, 8, 1), (0, 10, 1), (3, 1, 5), (0, 9, 1), (3, 2, 5), (0, 6, 3), (1, 6),
    (3, 3, 5), (0, 11, 0), (3, 4, 5), (4, 5), (0, 8, 2), (0, 7, 3), (1, 7), (0, 10, 2), (2, 6), (3, 1, 6),
    (0, 11, 1), (3, 4, 6), (3, 5, 6), (4, 6), (2, 7), (3, 0, 7), (3, 2, 7), (0, 8, 3), (1, 8), (3, 4, 7),
    (0, 9, 2), (0, 10, 3), (3, 5, 7), (0, 11, 2), (3, 6, 7), (4, 7), (2, 8), (3, 4, 8), (3, 7, 8), (4, 8),
    (5, 7, 0), (5, 7, 1), (2, 10), (3, 3, 10), (0, 9, 3), (1, 9), (3, 5, 10), (0, 11, 3), (3, 6, 10),
    (3, 8, 10), (4, 10), (5, 3, 0), (5, 3, 1), (5, 10, 0), (2, 9), (3, 0, 9), (3, 1, 9), (3, 2, 9), (3, 4, 9),
    (3, 5, 9), (3, 6, 9), (3, 8, 9), (4, 9), (5, 6, 0), (5, 6, 1), (5, 5, 0), (5, 5, 1), (5, 4, 0), (5, 4, 1),
    (5, 2, 0), (5, 2, 1), (5, 0, 1), (2, 11), (3, 1, 11), (3, 8, 11), (3, 9, 11), (4, 11), (5, 9, 0),
    (5, 9, 1), (5, 8, 0), (5, 8, 1), (5, 1, 0), (5, 1, 1), (5, 11, 0),
)
SLOTS = len(SPOTS)
SHARED = len(LEFT)
NT = (((1,), (1,)), ((), ()))


def place():
    owner, z = lax.axis_index("owner"), lax.axis_index("rep")
    return owner // (2 * SIDE), (owner // 2) % SIDE, owner % 2, z


def at(here, step, flip):
    x, y, core, z = here
    x = (x + step[0] + SIDE) % SIDE
    y = (y + step[1] + SIDE) % SIDE
    z = (z + step[2] + SIDE) % SIDE
    return ((x * SIDE + y) * 2 + (core + flip) % 2, z)


def kernel(
    emb_ref, cluster_ref, out_ref, rows, names, results, near, held, tall, wide,
    row_send, row_recv, name_send, name_recv, pair_send, pair_recv, pname_send, pname_recv,
    result_send, result_recv,
):
    here = place()
    core = here[2]
    count = emb_ref.shape[0]
    part = count // CHUNKS

    barrier = pltpu.get_barrier_semaphore()
    for step in STEPS:
        pl.semaphore_signal(barrier, 1, device_id=at(here, step, 0), device_id_type=MESH)
    pl.semaphore_signal(barrier, 1, device_id=at(here, (0, 0, 0), 1), device_id_type=MESH)

    values = emb_ref[...].astype(jnp.float32)
    factor = lax.rsqrt(jnp.mean(values * values, axis=1, keepdims=True) + 1e-06)
    rows[0, 0] = (values * (factor * emb_ref.shape[1] ** (-0.5))).astype(jnp.bfloat16)
    names[0, 0] = jnp.broadcast_to(cluster_ref[...].astype(jnp.float32), names.shape[2:])
    pl.semaphore_wait(barrier, len(STEPS) + 1)

    def chunk_copy(src, dst, chunk, step):
        span = pl.ds(chunk * part, part)
        return pltpu.make_async_remote_copy(
            rows.at[src, 0, span], rows.at[dst, 0, span], row_send, row_recv.at[dst, chunk],
            device_id=at(here, step, 0), device_id_type=MESH)

    def name_copy(src, dst, step):
        return pltpu.make_async_remote_copy(
            names.at[src, 0], names.at[dst, 0], name_send, name_recv.at[dst],
            device_id=at(here, step, 0), device_id_type=MESH)

    def pair_copy(slot):
        return pltpu.make_async_remote_copy(
            rows.at[slot, 0], rows.at[slot, 1], pair_send, pair_recv.at[slot],
            device_id=at(here, (0, 0, 0), 1), device_id_type=MESH)

    def pair_name_copy(slot):
        return pltpu.make_async_remote_copy(
            names.at[slot, 0], names.at[slot, 1], pname_send, pname_recv.at[slot],
            device_id=at(here, (0, 0, 0), 1), device_id_type=MESH)

    def result_copy(slot, side):
        back = tuple(-v for v in SPOTS[slot])
        return pltpu.make_async_remote_copy(
            held.at[side, slot], results.at[side, slot], result_send, result_recv.at[side],
            device_id=at(here, back, side), device_id_type=MESH)

    def forward(slot, chunk):
        for who in range(2):
            kids = [k for k in ORDER[who][chunk] if PARENT[who][chunk][k] == slot]
            if not kids:
                continue

            @pl.when(core == who)
            def _():
                for k in kids:
                    step = STEPS[WAY[who][chunk][k]]
                    chunk_copy(slot, k, chunk, step).start()
                    if chunk == 0:
                        name_copy(slot, k, step).start()

    def share(slot):
        pair_copy(slot).start()
        pair_name_copy(slot).start()

    joined = set()

    def join(slot):
        if slot not in joined:
            joined.add(slot)
            pair_copy(slot).wait_recv()
            pair_name_copy(slot).wait_recv()

    def open_step(slot):
        near[...] = jnp.broadcast_to(names[slot, 0, 0:1, :], (128, count)).T
        tall[...] = jnp.full(tall.shape, -1.0, jnp.float32)

    def pair(a, b):
        left = near[...]
        best = tall[...]
        both = rows[a].reshape(2 * count, rows.shape[3])
        scores = lax.dot_general(rows[b, 0], both, NT, preferred_element_type=jnp.float32)
        for side in range(2):
            for half in range(count // 128):
                low = half * 128
                tile = scores[:, side * count + low:side * count + low + 128]
                match = left == names[a, side, 0:1, low:low + 128]
                if a == b and side == 0:
                    i = lax.broadcasted_iota(jnp.int32, tile.shape, 0)
                    j = lax.broadcasted_iota(jnp.int32, tile.shape, 1) + low
                    match = match & (i != j)
                tile = jnp.where(match, tile, jnp.float32(-1.0))
                best = jnp.maximum(best, tile)
                if a != b:
                    up = jnp.max(tile.reshape(count // 8, 8, 128), axis=0)
                    held[side, a, :, low:low + 128] = jnp.maximum(held[side, a, :, low:low + 128], up)
        tall[...] = best

    def close_step(slot):
        flat = tall[...].T
        held[0, slot] = jnp.max(flat.reshape(128 // 8, 8, count), axis=0)
        if slot < SHARED:
            held[1, slot] = jnp.full(held.shape[2:], -1.0, jnp.float32)

    for chunk in range(CHUNKS):
        forward(0, chunk)
    share(0)
    for task in TASKS:
        kind = task[0]
        if kind == 0:
            slot, chunk = task[1:]
            chunk_copy(0, slot, chunk, STEPS[0]).wait_recv()
            if chunk == 0:
                name_copy(0, slot, STEPS[0]).wait_recv()
            forward(slot, chunk)
        elif kind == 1:
            share(task[1])
        elif kind == 2:
            open_step(task[1])
        elif kind == 3:
            join(task[1])
            pair(task[1], task[2])
        elif kind == 4:
            close_step(task[1])
        else:
            result_copy(task[1], task[2]).start()

    pltpu.make_async_remote_copy(
        results.at[0, 1:SLOTS], results.at[0, 1:SLOTS], result_send, result_recv.at[0],
        device_id=at(here, STEPS[0], 0), device_id_type=MESH).wait_recv()
    pltpu.make_async_remote_copy(
        results.at[1, 0:SHARED], results.at[1, 0:SHARED], result_send, result_recv.at[1],
        device_id=at(here, STEPS[0], 0), device_id_type=MESH).wait_recv()
    top = held[0, 0]
    for slot in range(1, SLOTS):
        top = jnp.maximum(top, results[0, slot])
    for slot in range(SHARED):
        top = jnp.maximum(top, results[1, slot])
    out_ref[...] = jnp.max(top, axis=0, keepdims=True)

    def drain(ref, sem):
        pltpu.make_async_remote_copy(
            ref, ref, sem, sem, device_id=at(here, STEPS[0], 0), device_id_type=MESH).wait_send()

    drain(rows.at[1:SLOTS, 0], row_send)
    drain(names.at[1:SLOTS, 0], name_send)
    drain(rows.at[0:SHARED, 0], pair_send)
    drain(names.at[0:SHARED, 0], pname_send)
    drain(results.at[0, 1:SLOTS], result_send)
    drain(results.at[0, 0:SHARED], result_send)


def on_device(embeddings, cluster):
    count, width = embeddings.shape
    dma = pltpu.SemaphoreType.DMA
    best = pl.pallas_call(
        kernel,
        out_shape=jax.ShapeDtypeStruct((1, count), jnp.float32),
        in_specs=[pl.BlockSpec(memory_space=pltpu.VMEM)] * 2,
        out_specs=pl.BlockSpec(memory_space=pltpu.VMEM),
        scratch_shapes=[
            pltpu.VMEM((SLOTS, 2, count, width), jnp.bfloat16),
            pltpu.VMEM((SLOTS, 2, 8, count), jnp.float32),
            pltpu.VMEM((2, SLOTS, 8, count), jnp.float32),
            pltpu.VMEM((count, 128), jnp.float32),
            pltpu.VMEM((2, SLOTS, 8, count), jnp.float32),
            pltpu.VMEM((count, 128), jnp.float32),
            pltpu.VMEM((8, count), jnp.float32),
            dma(()), dma((SLOTS, CHUNKS)), dma(()), dma((SLOTS,)),
            dma(()), dma((SLOTS,)), dma(()), dma((SLOTS,)),
            dma(()), dma((2,)),
        ],
        compiler_params=pltpu.CompilerParams(
            collective_id=0, has_side_effects=True, vmem_limit_bytes=48 * 2**20),
    )(embeddings, cluster.reshape(1, count))
    return best.reshape(count)


def solution(mesh):
    return jax.shard_map(
        on_device,
        mesh=mesh,
        in_specs=(P(("owner", "rep"), None), P(("owner", "rep"))),
        out_specs=P(("owner", "rep")),
        check_vma=False,
    )
```

```python
import jax
import jax.numpy as jnp
from jax import lax
from jax.experimental import pallas as pl
from jax.experimental.pallas import tpu as pltpu
from jax.sharding import PartitionSpec as P

MESH = pl.DeviceIdType.MESH
SIDE = 4
HOME = (0, 0, 0)
STEPS = ((1, 0, 0), (-1, 0, 0), (0, 1, 0), (0, -1, 0), (0, 0, 1), (0, 0, -1))
SPOTS = (
    ((0, 0, 0), (1, 0, 0), (3, 0, 0), (0, 1, 0), (0, 1, 1), (1, 3, 0), (3, 1, 0), (1, 0, 3), (1, 3, 1), (1, 1, 3), (1, 3, 2), (1, 1, 2)),
    ((0, 0, 0), (0, 0, 3), (0, 0, 1), (0, 3, 0), (1, 0, 1), (3, 3, 0), (0, 3, 3), (3, 2, 0), (2, 0, 1), (1, 3, 3), (0, 2, 3), (2, 2, 0)),
)
SHARED = ((0, 1, 2, 3, 4, 5, 6, 7, 8), (0, 1, 2, 3, 4, 5, 7, 8, 9, 11))
PARENT = (
    (
        (-1, 0, 0, 0, 3, 1, 2, 1, 5, 7, 8, 9),
        (-1, 0, 0, 0, 3, 1, 2, 1, 5, 7, 8, 9),
        (-1, 0, 0, 0, 3, 1, 2, 1, 5, 7, 8, 9),
        (-1, 0, 0, 0, 3, 1, 3, 1, 5, 7, 8, 9),
    ),
    (
        (-1, 0, 0, 0, 2, 3, 3, 5, 4, 6, 6, 7),
        (-1, 0, 0, 0, 2, 3, 3, 5, 4, 6, 6, 7),
        (-1, 0, 0, 0, 2, 3, 3, 5, 4, 6, 6, 7),
        (-1, 0, 0, 0, 2, 3, 3, 5, 4, 6, 6, 7),
    ),
)
WAY = (
    (
        (-1, 0, 1, 2, 4, 3, 2, 5, 4, 2, 4, 5),
        (-1, 0, 1, 2, 4, 3, 2, 5, 4, 2, 4, 5),
        (-1, 0, 1, 2, 4, 3, 2, 5, 4, 2, 4, 5),
        (-1, 0, 1, 2, 4, 3, 1, 5, 4, 2, 4, 5),
    ),
    (
        (-1, 5, 4, 3, 0, 1, 5, 3, 0, 0, 3, 1),
        (-1, 5, 4, 3, 0, 1, 5, 3, 0, 0, 3, 1),
        (-1, 5, 4, 3, 0, 1, 5, 3, 0, 0, 3, 1),
        (-1, 5, 4, 3, 0, 1, 5, 3, 0, 0, 3, 1),
    ),
)
ORDER = (
    (
        (5, 1, 7, 11, 2, 6, 9, 10, 3, 8, 4),
        (8, 1, 4, 7, 2, 10, 5, 3, 9, 6, 11),
        (7, 1, 5, 8, 9, 6, 11, 2, 3, 10, 4),
        (9, 2, 3, 5, 4, 8, 1, 11, 7, 10, 6),
    ),
    (
        (5, 3, 7, 2, 4, 1, 6, 8, 10, 9, 11),
        (1, 11, 3, 9, 2, 8, 6, 4, 10, 5, 7),
        (3, 7, 1, 4, 5, 2, 6, 9, 10, 8, 11),
        (3, 1, 5, 2, 8, 9, 10, 11, 7, 4, 6),
    ),
)
TASKS = (
    (
        (1, 0, 0), (2, 0, 0), (3, 0, 0), (4, 0, 0), (0, 1, 0), (0, 2, 0), (0, 3, 0), (2, 12, 0), (4, 12, 0),
        (0, 1, 1), (0, 2, 1), (0, 3, 1), (0, 1, 2), (0, 2, 2), (0, 3, 2), (0, 1, 3), (1, 1, 1), (0, 2, 3),
        (1, 2, 2), (0, 3, 3), (1, 3, 3), (2, 1, 0), (3, 12, 1), (3, 0, 1), (4, 1, 0), (2, 2, 0), (3, 12, 2),
        (3, 1, 2), (4, 2, 0), (0, 4, 0), (0, 5, 0), (0, 6, 0), (0, 7, 0), (2, 3, 0), (3, 12, 3), (3, 1, 3),
        (3, 0, 3), (3, 2, 3), (4, 3, 0), (0, 4, 1), (0, 5, 1), (0, 6, 1), (2, 13, 0), (3, 1, 13), (4, 13, 0),
        (2, 14, 0), (3, 2, 14), (4, 14, 0), (2, 15, 0), (3, 1, 15), (4, 15, 0), (0, 4, 2), (0, 5, 2),
        (0, 6, 2), (0, 7, 1), (0, 4, 3), (1, 4, 4), (0, 5, 3), (1, 5, 5), (0, 6, 3), (1, 6, 6), (2, 4, 0),
        (3, 1, 4), (3, 3, 4), (0, 9, 0), (3, 2, 4), (3, 13, 4), (3, 0, 4), (3, 15, 4), (4, 4, 0), (0, 7, 2),
        (0, 8, 0), (2, 5, 0), (3, 12, 5), (3, 3, 5), (3, 13, 5), (3, 14, 5), (3, 4, 5), (4, 5, 0), (5, 12, 0),
        (0, 8, 1), (2, 6, 0), (3, 1, 6), (3, 13, 6), (0, 9, 1), (3, 4, 6), (3, 15, 6), (3, 5, 6), (4, 6, 0),
        (5, 1, 0), (0, 7, 3), (1, 7, 7), (0, 8, 2), (2, 16, 0), (3, 5, 16), (3, 6, 16), (4, 16, 0),
        (2, 17, 0), (4, 17, 0), (2, 7, 0), (3, 4, 7), (0, 8, 3), (1, 8, 8), (3, 16, 7), (3, 14, 7), (3, 5, 7),
        (0, 9, 2), (3, 2, 7), (3, 15, 7), (3, 0, 7), (3, 6, 7), (4, 7, 0), (0, 10, 0), (0, 11, 0), (2, 8, 0),
        (3, 7, 8), (3, 16, 8), (3, 13, 8), (3, 2, 8), (3, 3, 8), (0, 10, 1), (0, 11, 1), (3, 0, 8), (3, 6, 8),
        (3, 17, 8), (4, 8, 0), (5, 7, 0), (5, 16, 0), (5, 13, 0), (0, 9, 3), (2, 9, 0), (3, 4, 9), (3, 8, 9),
        (0, 10, 2), (3, 14, 9), (3, 0, 9), (3, 5, 9), (3, 15, 9), (4, 9, 0), (5, 4, 0), (5, 8, 0), (5, 14, 0),
        (0, 11, 2), (0, 10, 3), (2, 18, 0), (3, 9, 18), (4, 18, 0), (2, 19, 0), (3, 9, 19), (4, 19, 0),
        (5, 9, 0), (5, 19, 0), (2, 10, 0), (3, 2, 10), (3, 3, 10), (3, 5, 10), (3, 6, 10), (3, 17, 10),
        (3, 18, 10), (4, 10, 0), (5, 2, 0), (5, 3, 0), (5, 5, 0), (0, 11, 3), (2, 20, 0), (4, 20, 0),
        (2, 11, 0), (3, 0, 11), (3, 6, 11), (3, 10, 11), (3, 20, 11), (3, 15, 11), (3, 17, 11), (3, 18, 11),
        (4, 11, 0), (5, 6, 0), (5, 10, 0), (5, 20, 0), (5, 15, 0), (5, 17, 0), (5, 18, 0), (2, 21, 0),
        (3, 11, 21), (4, 21, 0), (5, 11, 0), (5, 21, 0),
    ),
    (
        (1, 0, 0), (2, 0, 0), (3, 0, 0), (4, 0, 0), (0, 1, 0), (0, 2, 0), (0, 3, 0), (2, 12, 0), (3, 0, 12),
        (4, 12, 0), (0, 1, 1), (0, 2, 1), (0, 3, 1), (0, 1, 2), (0, 2, 2), (0, 3, 2), (0, 1, 3), (1, 1, 1),
        (0, 2, 3), (1, 2, 2), (0, 3, 3), (1, 3, 3), (2, 1, 0), (3, 12, 1), (3, 0, 1), (4, 1, 0), (2, 2, 0),
        (3, 12, 2), (3, 1, 2), (4, 2, 0), (5, 12, 0), (0, 4, 0), (0, 5, 0), (2, 3, 0), (3, 0, 3), (3, 2, 3),
        (3, 1, 3), (4, 3, 0), (0, 4, 1), (0, 5, 1), (0, 6, 0), (2, 13, 0), (3, 2, 13), (4, 13, 0), (2, 14, 0),
        (3, 3, 14), (3, 1, 14), (4, 14, 0), (0, 4, 2), (0, 5, 2), (2, 15, 0), (3, 3, 15), (3, 1, 15),
        (3, 2, 15), (4, 15, 0), (0, 4, 3), (1, 4, 4), (0, 6, 1), (2, 4, 0), (3, 14, 4), (3, 3, 4), (3, 15, 4),
        (3, 0, 4), (3, 1, 4), (3, 2, 4), (4, 4, 0), (5, 14, 0), (0, 5, 3), (1, 5, 5), (0, 7, 0), (0, 8, 0),
        (2, 5, 0), (3, 15, 5), (3, 13, 5), (3, 4, 5), (3, 0, 5), (3, 1, 5), (4, 5, 0), (0, 6, 2), (0, 9, 0),
        (0, 10, 0), (2, 16, 0), (3, 5, 16), (4, 16, 0), (2, 17, 0), (3, 5, 17), (4, 17, 0), (2, 18, 0),
        (4, 18, 0), (0, 7, 1), (0, 8, 1), (0, 6, 3), (0, 7, 2), (0, 8, 2), (2, 6, 0), (3, 5, 6), (3, 13, 6),
        (0, 11, 0), (3, 4, 6), (3, 18, 6), (3, 16, 6), (3, 2, 6), (4, 6, 0), (0, 9, 1), (0, 10, 1),
        (2, 19, 0), (4, 19, 0), (0, 7, 3), (1, 7, 6), (0, 8, 3), (1, 8, 7), (2, 20, 0), (4, 20, 0), (2, 7, 0),
        (3, 13, 7), (0, 11, 1), (3, 4, 7), (3, 20, 7), (3, 19, 7), (0, 9, 2), (0, 10, 2), (3, 0, 7),
        (3, 1, 7), (3, 2, 7), (4, 7, 0), (5, 13, 0), (0, 11, 2), (2, 8, 0), (3, 5, 8), (3, 6, 8), (0, 9, 3),
        (1, 9, 8), (0, 10, 3), (3, 20, 8), (3, 17, 8), (3, 19, 8), (3, 0, 8), (3, 1, 8), (3, 2, 8), (4, 8, 0),
        (5, 5, 0), (5, 6, 0), (5, 20, 0), (5, 17, 0), (2, 9, 0), (3, 7, 9), (3, 1, 9), (3, 2, 9), (3, 18, 9),
        (0, 11, 3), (1, 11, 9), (3, 16, 9), (4, 9, 0), (5, 7, 0), (2, 10, 0), (3, 1, 10), (3, 2, 10),
        (3, 4, 10), (3, 8, 10), (3, 18, 10), (3, 0, 10), (3, 15, 10), (3, 16, 10), (4, 10, 0), (5, 1, 0),
        (5, 2, 0), (5, 4, 0), (5, 8, 0), (5, 18, 0), (5, 10, 0), (2, 11, 0), (3, 0, 11), (3, 3, 11),
        (3, 9, 11), (3, 15, 11), (3, 16, 11), (3, 19, 11), (4, 11, 0), (5, 3, 0), (5, 9, 0), (5, 15, 0),
        (5, 16, 0), (5, 19, 0), (5, 11, 0),
    ),
)
SLOTS = len(SPOTS[0])
TAKEN = max(len(shared) for shared in SHARED)
NODES = SLOTS + TAKEN
CHUNKS = len(PARENT[0])
NT = (((1,), (1,)), ((), ()))


def place():
    owner, z = lax.axis_index("owner"), lax.axis_index("rep")
    return owner // (2 * SIDE), (owner // 2) % SIDE, owner % 2, z


def kernel(
    emb_ref, cluster_ref, out_ref, raw, label, rows, names, held, leaving, results, near, tall,
    load_sem, row_send, row_recv, name_send, name_recv, pair_send, pair_recv,
    pname_send, pname_recv, result_send, result_recv,
):
    x, y, core, z = place()
    count = raw.shape[0]
    part = count // CHUNKS

    def at(step, flip):
        dx, dy, dz = step
        spot = ((x + dx + SIDE) % SIDE * SIDE + (y + dy + SIDE) % SIDE) * 2 + (core + flip) % 2
        return spot, (z + dz + SIDE) % SIDE

    loads = (
        pltpu.make_async_copy(emb_ref, raw, load_sem.at[0]),
        pltpu.make_async_copy(cluster_ref, label, load_sem.at[1]),
    )
    for load in loads:
        load.start()
    barrier = pltpu.get_barrier_semaphore()
    near_by = [at(step, 0) for step in STEPS]
    twin = at(HOME, 1)
    for spot in near_by + [twin]:
        pl.semaphore_signal(barrier, 1, device_id=spot, device_id_type=MESH)
    for load in loads:
        load.wait()

    values = raw[...].astype(jnp.float32)
    factor = lax.rsqrt(jnp.mean(values * values, axis=1, keepdims=True) + 1e-06)
    rows[0] = (values * (factor * raw.shape[1] ** (-0.5))).astype(jnp.bfloat16)
    names[0] = jnp.broadcast_to(label[...].astype(jnp.float32), names.shape[1:])
    pl.semaphore_wait(barrier, len(STEPS) + 1)

    def remote(src, dst, send, recv, spot):
        return pltpu.make_async_remote_copy(
            src, dst, send, recv, device_id=spot, device_id_type=MESH)

    def chunk_copy(src, dst, chunk, spot):
        span = pl.ds(chunk * part, part)
        return remote(rows.at[src, span], rows.at[dst, span], row_send, row_recv.at[dst, chunk], spot)

    def name_copy(src, dst, spot):
        return remote(names.at[src], names.at[dst], name_send, name_recv.at[dst], spot)

    def pair_copy(slot, i):
        return remote(rows.at[slot], rows.at[SLOTS + i], pair_send, pair_recv.at[i], twin)

    def pair_name_copy(slot, i):
        return remote(names.at[slot], names.at[SLOTS + i], pname_send, pname_recv.at[i], twin)

    def result_copy(who, node):
        flip = int(node >= SLOTS)
        spot = SPOTS[1 - who][SHARED[1 - who][node - SLOTS]] if flip else SPOTS[who][node]
        return remote(leaving.at[node], results.at[node], result_send, result_recv.at[flip],
                      at(tuple(-v for v in spot), flip))

    def forward(who, slot, chunk):
        for k in ORDER[who][chunk]:
            if PARENT[who][chunk][k] == slot:
                spot = near_by[WAY[who][chunk][k]]
                chunk_copy(slot, k, chunk, spot).start()
                if chunk == 0:
                    name_copy(slot, k, spot).start()

    def open_step(b):
        near[...] = jnp.broadcast_to(names[b, 0:1, :], (128, count)).T
        tall[...] = jnp.full(tall.shape, -1.0, jnp.float32)

    def pair(a, b):
        left = near[...]
        best = tall[...]
        scores = lax.dot_general(rows[b], rows[a], NT, preferred_element_type=jnp.float32)
        for low in range(0, count, 128):
            tile = scores[:, low:low + 128]
            match = left == names[a, 0:1, low:low + 128]
            if a == b:
                i = lax.broadcasted_iota(jnp.int32, tile.shape, 0)
                j = lax.broadcasted_iota(jnp.int32, tile.shape, 1) + low
                match = match & (i != j)
            tile = jnp.where(match, tile, jnp.float32(-1.0))
            best = jnp.maximum(best, tile)
            if a != b:
                up = jnp.max(tile.reshape(count // 8, 8, 128), axis=0)
                held[a, :, low:low + 128] = jnp.maximum(held[a, :, low:low + 128], up)
        tall[...] = best

    def close_step(b):
        held[b] = jnp.max(tall[...].T.reshape(128 // 8, 8, count), axis=0)

    def program(who):
        for chunk in range(CHUNKS):
            forward(who, 0, chunk)
        for kind, one, two in TASKS[who]:
            if kind == 0:
                chunk_copy(0, one, two, twin).wait_recv()
                if two == 0:
                    name_copy(0, one, twin).wait_recv()
                forward(who, one, two)
            elif kind == 1:
                pair_copy(one, two).start()
                pair_name_copy(one, two).start()
            elif kind == 2:
                if one >= SLOTS:
                    pair_copy(0, one - SLOTS).wait_recv()
                    pair_name_copy(0, one - SLOTS).wait_recv()
                open_step(one)
            elif kind == 3:
                pair(one, two)
            elif kind == 4:
                close_step(one)
            else:
                leaving[one] = jnp.max(held[one], axis=0, keepdims=True)
                result_copy(who, one).start()

        given, taken = len(SHARED[who]), len(SHARED[1 - who])
        own, other = results.at[1:SLOTS], results.at[SLOTS:SLOTS + given]
        remote(own, own, result_send, result_recv.at[0], twin).wait_recv()
        remote(other, other, result_send, result_recv.at[1], twin).wait_recv()
        top = jnp.max(held[0], axis=0, keepdims=True)
        for node in range(1, SLOTS + given):
            top = jnp.maximum(top, results[node])
        out_ref[...] = top

        def drain(ref, sem):
            remote(ref, ref, sem, sem, twin).wait_send()

        drain(rows.at[1:SLOTS], row_send)
        drain(names.at[1:SLOTS], name_send)
        drain(rows.at[0:given], pair_send)
        drain(names.at[0:given], pname_send)
        drain(results.at[1:SLOTS + taken], result_send)

    for who in range(2):
        pl.when(core == who)(lambda who=who: program(who))


def on_device(embeddings, cluster):
    count, width = embeddings.shape
    dma = pltpu.SemaphoreType.DMA
    best = pl.pallas_call(
        kernel,
        out_shape=jax.ShapeDtypeStruct((1, count), jnp.float32),
        in_specs=[pl.BlockSpec(memory_space=pl.ANY)] * 2,
        out_specs=pl.BlockSpec(memory_space=pltpu.VMEM),
        scratch_shapes=[
            pltpu.VMEM((count, width), jnp.bfloat16),
            pltpu.VMEM((1, count), jnp.int32),
            pltpu.VMEM((NODES, count, width), jnp.bfloat16),
            pltpu.VMEM((NODES, 8, count), jnp.float32),
            pltpu.VMEM((NODES, 8, count), jnp.float32),
            pltpu.VMEM((NODES, 1, count), jnp.float32),
            pltpu.VMEM((NODES, 1, count), jnp.float32),
            pltpu.VMEM((count, 128), jnp.float32),
            pltpu.VMEM((count, 128), jnp.float32),
            dma((2,)), dma(()), dma((SLOTS, CHUNKS)), dma(()), dma((SLOTS,)),
            dma(()), dma((TAKEN,)), dma(()), dma((TAKEN,)),
            dma(()), dma((2,)),
        ],
        compiler_params=pltpu.CompilerParams(
            collective_id=0, has_side_effects=True, vmem_limit_bytes=56 * 2**20),
    )(embeddings, cluster.reshape(1, count))
    return best.reshape(count)


def solution(mesh):
    return jax.shard_map(
        on_device,
        mesh=mesh,
        in_specs=(P(("owner", "rep"), None), P(("owner", "rep"))),
        out_specs=P(("owner", "rep")),
        check_vma=False,
    )
```

```python
import jax
import jax.numpy as jnp
from jax import lax
from jax.experimental import pallas as pl
from jax.experimental.pallas import tpu as pltpu
from jax.sharding import PartitionSpec as P

MESH = pl.DeviceIdType.MESH
SIDE = 4
HOME = (0, 0, 0)
STEPS = ((1, 0, 0), (-1, 0, 0), (0, 1, 0), (0, -1, 0), (0, 0, 1), (0, 0, -1))
SPOTS = (
    ((0, 0, 0), (1, 0, 0), (3, 0, 0), (0, 1, 0), (0, 0, 1), (0, 1, 3), (3, 3, 0), (0, 2, 3), (0, 0, 2), (2, 0, 0), (0, 2, 2), (2, 3, 0)),
    ((0, 0, 0), (0, 0, 3), (0, 3, 0), (1, 3, 0), (0, 1, 3), (2, 3, 0), (3, 3, 0), (0, 3, 1), (0, 1, 2), (2, 2, 0), (0, 3, 2), (3, 2, 0)),
)
SHARED = ((0, 1, 2, 3, 4, 5, 6, 7, 8), (0, 1, 2, 3, 4, 5, 6, 7, 8, 9, 11))
PARENT = (
    (
        (-1, 0, 0, 0, 0, 3, 2, 5, 4, 2, 7, 6),
        (-1, 0, 0, 0, 0, 3, 2, 5, 4, 2, 7, 6),
        (-1, 0, 0, 0, 0, 3, 2, 5, 4, 2, 7, 6),
        (-1, 0, 0, 0, 0, 3, 2, 5, 4, 2, 7, 6),
    ),
    (
        (-1, 0, 0, 2, 1, 6, 2, 2, 4, 11, 7, 6),
        (-1, 0, 0, 2, 1, 3, 2, 2, 4, 5, 7, 6),
        (-1, 0, 0, 2, 1, 3, 2, 2, 4, 5, 7, 6),
        (-1, 0, 0, 2, 1, 3, 2, 2, 4, 5, 7, 6),
    ),
)
WAY = (
    (
        (-1, 0, 1, 2, 4, 5, 3, 2, 4, 1, 5, 1),
        (-1, 0, 1, 2, 4, 5, 3, 2, 4, 1, 5, 1),
        (-1, 0, 1, 2, 4, 5, 3, 2, 4, 1, 5, 1),
        (-1, 0, 1, 2, 4, 5, 3, 2, 4, 1, 5, 1),
    ),
    (
        (-1, 5, 3, 0, 2, 1, 1, 4, 5, 1, 4, 3),
        (-1, 5, 3, 0, 2, 0, 1, 4, 5, 3, 4, 3),
        (-1, 5, 3, 0, 2, 0, 1, 4, 5, 3, 4, 3),
        (-1, 5, 3, 0, 2, 0, 1, 4, 5, 3, 4, 3),
    ),
)
ORDER = (
    (
        (2, 8, 9, 1, 7, 4, 11, 5, 6, 10, 3),
        (3, 10, 11, 2, 4, 7, 1, 5, 6, 9, 8),
        (9, 5, 1, 3, 11, 7, 10, 2, 8, 4, 6),
        (7, 5, 8, 11, 3, 1, 6, 2, 4, 9, 10),
    ),
    (
        (11, 4, 2, 10, 5, 9, 1, 8, 3, 6, 7),
        (2, 3, 10, 9, 8, 4, 1, 5, 7, 11, 6),
        (11, 5, 3, 9, 7, 2, 6, 8, 10, 1, 4),
        (8, 2, 11, 1, 9, 7, 6, 4, 3, 10, 5),
    ),
)
TASKS = (
    (
        (1, 0, 0), (2, 0, 0), (3, 0, 0), (4, 0, 0), (0, 2, 0), (0, 3, 0), (0, 4, 0), (2, 12, 0), (4, 12, 0),
        (0, 2, 1), (0, 3, 1), (0, 4, 1), (0, 2, 2), (0, 3, 2), (0, 4, 2), (0, 5, 0), (0, 6, 0), (0, 2, 3),
        (0, 3, 3), (0, 4, 3), (0, 1, 0), (0, 1, 1), (0, 1, 2), (0, 1, 3), (1, 1, 1), (2, 1, 0), (3, 0, 1),
        (1, 2, 2), (1, 3, 3), (1, 4, 4), (3, 12, 1), (4, 1, 0), (2, 2, 0), (3, 12, 2), (0, 5, 1), (0, 6, 1),
        (3, 1, 2), (4, 2, 0), (2, 3, 0), (3, 0, 3), (3, 2, 3), (3, 1, 3), (4, 3, 0), (2, 4, 0), (3, 0, 4),
        (0, 5, 2), (0, 6, 2), (3, 12, 4), (3, 2, 4), (3, 3, 4), (3, 1, 4), (4, 4, 0), (2, 13, 0), (3, 2, 13),
        (3, 3, 13), (3, 4, 13), (3, 1, 13), (4, 13, 0), (2, 14, 0), (3, 2, 14), (0, 7, 0), (3, 3, 14),
        (3, 1, 14), (4, 14, 0), (0, 5, 3), (0, 6, 3), (1, 5, 5), (2, 5, 0), (3, 2, 5), (1, 6, 6), (3, 12, 5),
        (0, 7, 1), (3, 14, 5), (3, 1, 5), (3, 4, 5), (4, 5, 0), (5, 2, 0), (2, 6, 0), (3, 12, 6), (3, 3, 6),
        (3, 13, 6), (0, 7, 2), (3, 1, 6), (3, 5, 6), (3, 4, 6), (4, 6, 0), (5, 12, 0), (2, 15, 0), (3, 5, 15),
        (3, 6, 15), (4, 15, 0), (2, 16, 0), (3, 6, 16), (4, 16, 0), (0, 7, 3), (1, 7, 7), (2, 7, 0),
        (3, 0, 7), (0, 8, 0), (0, 8, 1), (0, 8, 2), (0, 8, 3), (1, 8, 8), (3, 14, 7), (3, 15, 7), (3, 4, 7),
        (3, 1, 7), (3, 6, 7), (4, 7, 0), (2, 8, 0), (3, 0, 8), (3, 14, 8), (3, 15, 8), (3, 1, 8), (3, 5, 8),
        (3, 6, 8), (3, 13, 8), (4, 8, 0), (5, 15, 0), (5, 14, 0), (2, 17, 0), (3, 7, 17), (3, 8, 17),
        (4, 17, 0), (5, 17, 0), (2, 18, 0), (3, 7, 18), (3, 8, 18), (4, 18, 0), (5, 18, 0), (2, 19, 0),
        (4, 19, 0), (0, 9, 0), (0, 9, 1), (0, 9, 2), (0, 9, 3), (2, 9, 0), (3, 5, 9), (3, 7, 9), (3, 13, 9),
        (3, 19, 9), (3, 16, 9), (3, 4, 9), (3, 8, 9), (4, 9, 0), (5, 7, 0), (5, 5, 0), (5, 16, 0), (5, 19, 0),
        (5, 13, 0), (2, 20, 0), (3, 9, 20), (4, 20, 0), (5, 20, 0), (0, 10, 0), (0, 10, 1), (0, 10, 2),
        (0, 10, 3), (2, 10, 0), (3, 1, 10), (3, 6, 10), (3, 9, 10), (3, 8, 10), (4, 10, 0), (5, 6, 0),
        (5, 9, 0), (5, 1, 0), (2, 21, 0), (3, 10, 21), (4, 21, 0), (5, 21, 0), (2, 22, 0), (3, 10, 22),
        (4, 22, 0), (5, 10, 0), (5, 22, 0), (0, 11, 0), (0, 11, 1), (0, 11, 2), (0, 11, 3), (2, 11, 0),
        (3, 3, 11), (3, 4, 11), (3, 8, 11), (4, 11, 0), (5, 11, 0), (5, 8, 0), (5, 3, 0), (5, 4, 0),
    ),
    (
        (1, 0, 0), (2, 0, 0), (3, 0, 0), (4, 0, 0), (0, 1, 0), (0, 2, 0), (2, 12, 0), (3, 0, 12), (4, 12, 0),
        (0, 1, 1), (0, 2, 1), (0, 1, 2), (0, 2, 2), (0, 4, 0), (0, 6, 0), (0, 7, 0), (0, 1, 3), (0, 2, 3),
        (1, 1, 1), (2, 1, 0), (3, 0, 1), (4, 1, 0), (1, 2, 2), (2, 2, 0), (3, 12, 2), (0, 3, 1), (0, 4, 1),
        (3, 0, 2), (3, 1, 2), (4, 2, 0), (0, 6, 1), (0, 7, 1), (2, 13, 0), (4, 13, 0), (2, 14, 0), (4, 14, 0),
        (0, 3, 2), (0, 4, 2), (2, 15, 0), (4, 15, 0), (2, 16, 0), (4, 16, 0), (0, 3, 3), (0, 6, 2), (0, 7, 2),
        (0, 3, 0), (1, 3, 3), (2, 3, 0), (3, 14, 3), (0, 11, 0), (3, 2, 3), (0, 4, 3), (3, 0, 3), (3, 1, 3),
        (0, 5, 1), (3, 15, 3), (3, 16, 3), (4, 3, 0), (1, 4, 4), (2, 4, 0), (3, 12, 4), (3, 2, 4), (3, 13, 4),
        (3, 3, 4), (0, 5, 2), (3, 16, 4), (4, 4, 0), (5, 12, 0), (2, 17, 0), (4, 17, 0), (2, 18, 0),
        (4, 18, 0), (0, 5, 3), (0, 5, 0), (1, 5, 5), (2, 5, 0), (3, 2, 5), (0, 6, 3), (0, 7, 3), (3, 0, 5),
        (3, 1, 5), (3, 16, 5), (3, 15, 5), (1, 6, 6), (1, 7, 7), (3, 17, 5), (3, 4, 5), (4, 5, 0), (2, 6, 0),
        (3, 0, 6), (3, 1, 6), (3, 16, 6), (0, 8, 0), (0, 8, 1), (0, 8, 2), (0, 8, 3), (1, 8, 8), (3, 15, 6),
        (3, 17, 6), (3, 4, 6), (4, 6, 0), (2, 7, 0), (3, 6, 7), (3, 1, 7), (3, 17, 7), (3, 13, 7), (3, 14, 7),
        (3, 4, 7), (3, 3, 7), (3, 5, 7), (3, 18, 7), (4, 7, 0), (5, 6, 0), (0, 9, 1), (0, 9, 2), (0, 9, 0),
        (0, 9, 3), (1, 9, 9), (2, 8, 0), (3, 13, 8), (3, 14, 8), (3, 3, 8), (3, 5, 8), (3, 18, 8), (4, 8, 0),
        (5, 13, 0), (5, 14, 0), (2, 19, 0), (4, 19, 0), (0, 11, 1), (0, 11, 2), (0, 11, 3), (1, 11, 10),
        (2, 20, 0), (3, 8, 20), (4, 20, 0), (2, 9, 0), (3, 0, 9), (3, 4, 9), (3, 19, 9), (3, 16, 9),
        (3, 20, 9), (3, 15, 9), (3, 8, 9), (4, 9, 0), (5, 9, 0), (0, 10, 0), (0, 10, 1), (0, 10, 2),
        (0, 10, 3), (2, 10, 0), (3, 1, 10), (3, 2, 10), (3, 3, 10), (3, 5, 10), (3, 17, 10), (3, 18, 10),
        (3, 8, 10), (4, 10, 0), (5, 5, 0), (5, 3, 0), (5, 17, 0), (5, 18, 0), (5, 1, 0), (5, 2, 0),
        (2, 11, 0), (3, 0, 11), (3, 4, 11), (3, 7, 11), (3, 8, 11), (3, 10, 11), (3, 19, 11), (3, 16, 11),
        (3, 20, 11), (3, 15, 11), (4, 11, 0), (5, 8, 0), (5, 10, 0), (5, 11, 0), (5, 19, 0), (5, 4, 0),
        (5, 7, 0), (5, 20, 0), (5, 15, 0), (5, 16, 0),
    ),
)
SLOTS = len(SPOTS[0])
TAKEN = max(len(shared) for shared in SHARED)
NODES = SLOTS + TAKEN
CHUNKS = len(PARENT[0])
NT = (((1,), (1,)), ((), ()))


def place():
    owner, z = lax.axis_index("owner"), lax.axis_index("rep")
    return owner // (2 * SIDE), (owner // 2) % SIDE, owner % 2, z


def kernel(
    emb_ref, cluster_ref, out_ref, raw, label, rows, names, held, leaving, results, near, tall,
    load_sem, row_send, row_recv, name_send, name_recv, pair_send, pair_recv,
    pname_send, pname_recv, result_send, result_recv,
):
    x, y, core, z = place()
    count = raw.shape[0]
    part = count // CHUNKS

    def wrap(v):
        return jnp.where(v >= SIDE, v - SIDE, v)

    def at(step, flip):
        nx, ny, nz = (wrap(v + d % SIDE) for v, d in zip((x, y, z), step))
        return (nx * SIDE + ny) * 2 + (1 - core if flip else core), nz

    loads = (
        pltpu.make_async_copy(emb_ref, raw, load_sem.at[0]),
        pltpu.make_async_copy(cluster_ref, label, load_sem.at[1]),
    )
    for load in loads:
        load.start()
    barrier = pltpu.get_barrier_semaphore()
    near_by = [at(step, 0) for step in STEPS]
    twin = at(HOME, 1)
    for spot in near_by + [twin]:
        pl.semaphore_signal(barrier, 1, device_id=spot, device_id_type=MESH)
    homes = [[
        at(tuple(-v for v in SPOTS[who][node]), 0) if node < SLOTS else
        at(tuple(-v for v in SPOTS[1 - who][SHARED[1 - who][node - SLOTS]]), 1)
        for node in range(SLOTS + len(SHARED[1 - who]))] for who in range(2)]
    for load in loads:
        load.wait()

    values = raw[...].astype(jnp.float32)
    factor = lax.rsqrt(jnp.mean(values * values, axis=1, keepdims=True) + 1e-06)
    rows[0] = (values * (factor * raw.shape[1] ** (-0.5))).astype(jnp.bfloat16)
    names[0] = jnp.broadcast_to(label[...].astype(jnp.float32), names.shape[1:])
    pl.semaphore_wait(barrier, len(STEPS) + 1)

    def remote(src, dst, send, recv, spot):
        return pltpu.make_async_remote_copy(
            src, dst, send, recv, device_id=spot, device_id_type=MESH)

    def chunk_copy(src, dst, chunk, spot):
        span = pl.ds(chunk * part, part)
        return remote(rows.at[src, span], rows.at[dst, span], row_send, row_recv.at[dst, chunk], spot)

    def name_copy(src, dst, spot):
        return remote(names.at[src], names.at[dst], name_send, name_recv.at[dst], spot)

    def pair_copy(slot, i):
        return remote(rows.at[slot], rows.at[SLOTS + i], pair_send, pair_recv.at[i], twin)

    def pair_name_copy(slot, i):
        return remote(names.at[slot], names.at[SLOTS + i], pname_send, pname_recv.at[i], twin)

    def result_copy(who, node):
        flip = int(node >= SLOTS)
        return remote(leaving.at[node], results.at[node], result_send, result_recv.at[flip],
                      homes[who][node])

    def forward(who, slot, chunk):
        for k in ORDER[who][chunk]:
            if PARENT[who][chunk][k] == slot:
                spot = near_by[WAY[who][chunk][k]]
                chunk_copy(slot, k, chunk, spot).start()
                if chunk == 0:
                    name_copy(slot, k, spot).start()

    def open_step(b):
        near[...] = jnp.broadcast_to(names[b, 0:1, :], (128, count)).T
        tall[...] = jnp.full(tall.shape, -1.0, jnp.float32)

    def pair(a, b):
        left = near[...]
        best = tall[...]
        scores = lax.dot_general(rows[b], rows[a], NT, preferred_element_type=jnp.float32)
        for low in range(0, count, 128):
            tile = scores[:, low:low + 128]
            match = left == names[a, 0:1, low:low + 128]
            if a == b:
                i = lax.broadcasted_iota(jnp.int32, tile.shape, 0)
                j = lax.broadcasted_iota(jnp.int32, tile.shape, 1) + low
                match = match & (i != j)
            tile = jnp.where(match, tile, jnp.float32(-1.0))
            best = jnp.maximum(best, tile)
            if a != b:
                up = jnp.max(tile.reshape(count // 8, 8, 128), axis=0)
                held[a, :, low:low + 128] = jnp.maximum(held[a, :, low:low + 128], up)
        tall[...] = best

    def close_step(b):
        held[b] = jnp.max(tall[...].T.reshape(128 // 8, 8, count), axis=0)

    def program(who):
        for chunk in range(CHUNKS):
            forward(who, 0, chunk)
        for kind, one, two in TASKS[who]:
            if kind == 0:
                chunk_copy(0, one, two, twin).wait_recv()
                if two == 0:
                    name_copy(0, one, twin).wait_recv()
                forward(who, one, two)
            elif kind == 1:
                pair_copy(one, two).start()
                pair_name_copy(one, two).start()
            elif kind == 2:
                if one >= SLOTS:
                    pair_copy(0, one - SLOTS).wait_recv()
                    pair_name_copy(0, one - SLOTS).wait_recv()
                open_step(one)
            elif kind == 3:
                pair(one, two)
            elif kind == 4:
                close_step(one)
            else:
                leaving[one] = jnp.max(held[one], axis=0, keepdims=True)
                result_copy(who, one).start()

        given, taken = len(SHARED[who]), len(SHARED[1 - who])
        own, other = results.at[1:SLOTS], results.at[SLOTS:SLOTS + given]
        remote(own, own, result_send, result_recv.at[0], twin).wait_recv()
        remote(other, other, result_send, result_recv.at[1], twin).wait_recv()
        top = jnp.max(held[0], axis=0, keepdims=True)
        for node in range(1, SLOTS + given):
            top = jnp.maximum(top, results[node])
        out_ref[...] = top

        def drain(ref, sem):
            remote(ref, ref, sem, sem, twin).wait_send()

        drain(rows.at[1:SLOTS], row_send)
        drain(names.at[1:SLOTS], name_send)
        drain(rows.at[0:given], pair_send)
        drain(names.at[0:given], pname_send)
        drain(results.at[1:SLOTS + taken], result_send)

    for who in range(2):
        pl.when(core == who)(lambda who=who: program(who))


def on_device(embeddings, cluster):
    count, width = embeddings.shape
    dma = pltpu.SemaphoreType.DMA
    best = pl.pallas_call(
        kernel,
        out_shape=jax.ShapeDtypeStruct((1, count), jnp.float32),
        in_specs=[pl.BlockSpec(memory_space=pl.ANY)] * 2,
        out_specs=pl.BlockSpec(memory_space=pltpu.VMEM),
        scratch_shapes=[
            pltpu.VMEM((count, width), jnp.bfloat16),
            pltpu.VMEM((1, count), jnp.int32),
            pltpu.VMEM((NODES, count, width), jnp.bfloat16),
            pltpu.VMEM((NODES, 8, count), jnp.float32),
            pltpu.VMEM((NODES, 8, count), jnp.float32),
            pltpu.VMEM((NODES, 1, count), jnp.float32),
            pltpu.VMEM((NODES, 1, count), jnp.float32),
            pltpu.VMEM((count, 128), jnp.float32),
            pltpu.VMEM((count, 128), jnp.float32),
            dma((2,)), dma(()), dma((SLOTS, CHUNKS)), dma(()), dma((SLOTS,)),
            dma(()), dma((TAKEN,)), dma(()), dma((TAKEN,)),
            dma(()), dma((2,)),
        ],
        compiler_params=pltpu.CompilerParams(
            collective_id=0, has_side_effects=True, vmem_limit_bytes=56 * 2**20),
    )(embeddings, cluster.reshape(1, count))
    return best.reshape(count)


def solution(mesh):
    return jax.shard_map(
        on_device,
        mesh=mesh,
        in_specs=(P(("owner", "rep"), None), P(("owner", "rep"))),
        out_specs=P(("owner", "rep")),
        check_vma=False,
    )
```

```python
import jax
import jax.numpy as jnp
from jax import lax
from jax.experimental import pallas as pl
from jax.experimental.pallas import tpu as pltpu
from jax.sharding import PartitionSpec as P

MESH = pl.DeviceIdType.MESH
SIDE = 4
HOME = (0, 0, 0)
STEPS = ((1, 0, 0), (-1, 0, 0), (0, 1, 0), (0, -1, 0), (0, 0, 1), (0, 0, -1))
SPOTS = (
    ((0, 0, 0), (1, 0, 0), (0, 1, 0), (0, 0, 1), (1, 3, 0), (2, 0, 0), (0, 1, 3), (0, 0, 2), (0, 2, 0), (3, 1, 3), (2, 3, 0), (3, 1, 2)),
    ((0, 0, 0), (3, 0, 0), (0, 0, 3), (0, 3, 0), (2, 0, 0), (0, 1, 3), (0, 3, 1), (0, 0, 2), (2, 3, 0), (1, 1, 3), (3, 0, 2), (2, 2, 0)),
)
SHARED = ((0, 1, 2, 3, 4, 5, 6, 7, 8, 9), (0, 1, 2, 3, 4, 5, 6, 7, 8))
PARENT = (
    (
        (-1, 0, 0, 0, 1, 1, 2, 3, 2, 6, 4, 9),
        (-1, 0, 0, 0, 1, 1, 2, 3, 2, 6, 4, 9),
        (-1, 0, 0, 0, 1, 1, 2, 3, 2, 6, 4, 9),
        (-1, 0, 0, 0, 1, 1, 2, 3, 2, 6, 4, 9),
    ),
    (
        (-1, 0, 0, 0, 1, 2, 3, 2, 4, 5, 7, 8),
        (-1, 0, 0, 0, 1, 2, 3, 2, 4, 5, 7, 8),
        (-1, 0, 0, 0, 1, 2, 3, 2, 4, 5, 7, 8),
        (-1, 0, 0, 0, 1, 2, 3, 2, 4, 5, 7, 8),
    ),
)
WAY = (
    (
        (-1, 0, 2, 4, 3, 0, 5, 4, 2, 1, 0, 5),
        (-1, 0, 2, 4, 3, 0, 5, 4, 2, 1, 0, 5),
        (-1, 0, 2, 4, 3, 0, 5, 4, 2, 1, 0, 5),
        (-1, 0, 2, 4, 3, 0, 5, 4, 2, 1, 0, 5),
    ),
    (
        (-1, 1, 5, 3, 1, 2, 4, 5, 3, 0, 1, 3),
        (-1, 1, 5, 3, 1, 2, 4, 5, 3, 0, 1, 3),
        (-1, 1, 5, 3, 1, 2, 4, 5, 3, 0, 1, 3),
        (-1, 1, 5, 3, 1, 2, 4, 5, 3, 0, 1, 3),
    ),
)
ORDER = (
    (
        (2, 1, 6, 3, 4, 9, 5, 7, 8, 10, 11),
        (2, 1, 6, 3, 4, 9, 5, 7, 8, 10, 11),
        (2, 1, 6, 3, 4, 9, 5, 7, 8, 10, 11),
        (2, 1, 6, 3, 4, 9, 5, 7, 8, 10, 11),
    ),
    (
        (1, 2, 4, 3, 5, 7, 8, 6, 9, 10, 11),
        (1, 2, 4, 3, 5, 7, 8, 6, 9, 10, 11),
        (1, 2, 4, 3, 5, 7, 8, 6, 9, 10, 11),
        (1, 2, 4, 3, 5, 7, 8, 6, 9, 10, 11),
    ),
)
TASKS = (
    (
        (1, 0, 0), (2, 0, 0), (3, 0, 0), (4, 0, 0), (0, 1, 0), (0, 2, 0), (0, 3, 0), (2, 12, 0), (3, 0, 12),
        (4, 12, 0), (0, 1, 1), (0, 2, 1), (0, 3, 1), (0, 1, 2), (0, 2, 2), (0, 3, 2), (0, 1, 3), (1, 1, 1),
        (2, 1, 0), (3, 0, 1), (4, 1, 0), (0, 4, 0), (0, 6, 0), (0, 2, 3), (0, 3, 3), (1, 2, 2), (1, 3, 3),
        (2, 2, 0), (3, 12, 2), (3, 0, 2), (3, 1, 2), (4, 2, 0), (2, 3, 0), (3, 0, 3), (3, 1, 3), (3, 2, 3),
        (4, 3, 0), (0, 4, 1), (2, 13, 0), (3, 1, 13), (4, 13, 0), (0, 6, 1), (2, 14, 0), (4, 14, 0),
        (0, 4, 2), (2, 15, 0), (3, 2, 15), (4, 15, 0), (0, 6, 2), (0, 4, 3), (0, 9, 0), (1, 4, 4), (2, 4, 0),
        (3, 2, 4), (3, 12, 4), (3, 14, 4), (3, 3, 4), (3, 13, 4), (4, 4, 0), (0, 5, 0), (0, 5, 1), (0, 5, 2),
        (0, 5, 3), (1, 5, 5), (2, 5, 0), (3, 2, 5), (3, 0, 5), (3, 14, 5), (3, 3, 5), (3, 15, 5), (3, 13, 5),
        (3, 4, 5), (4, 5, 0), (0, 6, 3), (0, 9, 1), (1, 6, 6), (2, 6, 0), (3, 1, 6), (3, 3, 6), (3, 13, 6),
        (3, 4, 6), (3, 5, 6), (4, 6, 0), (2, 16, 0), (4, 16, 0), (0, 7, 0), (0, 7, 1), (0, 7, 2), (0, 7, 3),
        (1, 7, 7), (0, 8, 0), (0, 8, 1), (0, 8, 2), (0, 8, 3), (1, 8, 8), (2, 7, 0), (3, 1, 7), (3, 0, 7),
        (3, 6, 7), (3, 14, 7), (3, 13, 7), (3, 16, 7), (3, 4, 7), (3, 15, 7), (3, 5, 7), (4, 7, 0), (5, 1, 0),
        (0, 9, 2), (2, 8, 0), (3, 0, 8), (3, 14, 8), (3, 13, 8), (3, 16, 8), (3, 3, 8), (3, 15, 8), (3, 5, 8),
        (3, 7, 8), (4, 8, 0), (5, 16, 0), (5, 13, 0), (5, 14, 0), (0, 9, 3), (2, 17, 0), (3, 7, 17),
        (4, 17, 0), (1, 9, 9), (2, 18, 0), (3, 6, 18), (4, 18, 0), (5, 6, 0), (2, 19, 0), (4, 19, 0),
        (2, 9, 0), (3, 2, 9), (3, 8, 9), (3, 15, 9), (3, 4, 9), (3, 5, 9), (3, 19, 9), (3, 12, 9), (3, 18, 9),
        (4, 9, 0), (5, 8, 0), (5, 2, 0), (5, 15, 0), (2, 20, 0), (3, 9, 20), (4, 20, 0), (5, 20, 0),
        (0, 10, 0), (0, 10, 1), (0, 10, 2), (0, 10, 3), (2, 10, 0), (3, 7, 10), (3, 3, 10), (3, 9, 10),
        (3, 19, 10), (3, 18, 10), (3, 17, 10), (4, 10, 0), (5, 9, 0), (5, 7, 0), (5, 19, 0), (5, 3, 0),
        (0, 11, 0), (0, 11, 1), (0, 11, 2), (0, 11, 3), (2, 11, 0), (3, 4, 11), (3, 5, 11), (3, 10, 11),
        (3, 17, 11), (3, 12, 11), (3, 18, 11), (4, 11, 0), (5, 11, 0), (5, 10, 0), (5, 4, 0), (5, 5, 0),
        (5, 17, 0), (5, 18, 0), (5, 12, 0),
    ),
    (
        (1, 0, 0), (2, 0, 0), (3, 0, 0), (4, 0, 0), (0, 1, 0), (0, 2, 0), (0, 3, 0), (2, 12, 0), (4, 12, 0),
        (0, 1, 1), (0, 2, 1), (0, 3, 1), (0, 1, 2), (0, 2, 2), (0, 3, 2), (0, 1, 3), (1, 1, 1), (2, 1, 0),
        (3, 12, 1), (3, 0, 1), (4, 1, 0), (0, 5, 0), (0, 2, 3), (0, 3, 3), (0, 4, 0), (1, 2, 2), (1, 3, 3),
        (2, 2, 0), (3, 12, 2), (3, 0, 2), (3, 1, 2), (4, 2, 0), (2, 3, 0), (3, 0, 3), (3, 1, 3), (3, 2, 3),
        (4, 3, 0), (0, 4, 1), (2, 13, 0), (3, 3, 13), (3, 2, 13), (4, 13, 0), (0, 5, 1), (0, 7, 0),
        (2, 14, 0), (3, 2, 14), (4, 14, 0), (2, 15, 0), (3, 2, 15), (4, 15, 0), (0, 4, 2), (0, 5, 2),
        (0, 7, 1), (0, 8, 0), (0, 4, 3), (1, 4, 4), (2, 4, 0), (3, 0, 4), (3, 2, 4), (3, 3, 4), (4, 4, 0),
        (0, 8, 1), (0, 5, 3), (0, 7, 2), (2, 16, 0), (3, 4, 16), (4, 16, 0), (1, 5, 5), (0, 6, 0), (0, 6, 1),
        (0, 6, 2), (0, 6, 3), (1, 6, 6), (2, 5, 0), (3, 4, 5), (3, 3, 5), (3, 12, 5), (3, 15, 5), (3, 16, 5),
        (3, 1, 5), (4, 5, 0), (0, 8, 2), (0, 7, 3), (2, 6, 0), (3, 2, 6), (3, 12, 6), (3, 16, 6), (3, 14, 6),
        (3, 1, 6), (3, 5, 6), (4, 6, 0), (1, 7, 7), (2, 17, 0), (3, 6, 17), (3, 5, 17), (4, 17, 0), (0, 8, 3),
        (2, 18, 0), (4, 18, 0), (1, 8, 8), (2, 7, 0), (3, 16, 7), (3, 0, 7), (3, 4, 7), (3, 5, 7), (3, 1, 7),
        (4, 7, 0), (5, 16, 0), (2, 19, 0), (4, 19, 0), (2, 20, 0), (4, 20, 0), (2, 8, 0), (3, 5, 8),
        (3, 1, 8), (3, 15, 8), (3, 13, 8), (3, 7, 8), (3, 19, 8), (3, 18, 8), (4, 8, 0), (5, 5, 0), (0, 9, 0),
        (0, 9, 1), (0, 9, 2), (0, 9, 3), (2, 9, 0), (3, 12, 9), (3, 15, 9), (3, 3, 9), (3, 7, 9), (3, 6, 9),
        (3, 8, 9), (3, 14, 9), (3, 19, 9), (4, 9, 0), (5, 15, 0), (5, 12, 0), (2, 21, 0), (4, 21, 0),
        (0, 10, 0), (0, 10, 1), (0, 10, 2), (0, 10, 3), (2, 10, 0), (3, 2, 10), (3, 3, 10), (3, 9, 10),
        (3, 6, 10), (3, 8, 10), (3, 14, 10), (3, 20, 10), (3, 17, 10), (3, 18, 10), (4, 10, 0), (5, 8, 0),
        (5, 9, 0), (5, 10, 0), (5, 6, 0), (5, 17, 0), (5, 20, 0), (5, 2, 0), (5, 3, 0), (5, 14, 0),
        (0, 11, 0), (0, 11, 1), (0, 11, 2), (0, 11, 3), (2, 11, 0), (3, 0, 11), (3, 1, 11), (3, 4, 11),
        (3, 7, 11), (3, 21, 11), (3, 19, 11), (3, 18, 11), (3, 13, 11), (4, 11, 0), (5, 11, 0), (5, 21, 0),
        (5, 4, 0), (5, 7, 0), (5, 18, 0), (5, 19, 0), (5, 1, 0), (5, 13, 0),
    ),
)
SLOTS = len(SPOTS[0])
TAKEN = max(len(shared) for shared in SHARED)
NODES = SLOTS + TAKEN
CHUNKS = len(PARENT[0])
NT = (((1,), (1,)), ((), ()))


def place():
    owner, z = lax.axis_index("owner"), lax.axis_index("rep")
    return owner // (2 * SIDE), (owner // 2) % SIDE, owner % 2, z


def kernel(
    emb_ref, cluster_ref, out_ref, raw, label, rows, names, held, leaving, results,
    load_sem, row_send, row_recv, name_send, name_recv, pair_send, pair_recv,
    pname_send, pname_recv, result_send, result_recv,
):
    x, y, core, z = place()
    count = raw.shape[0]
    part = count // CHUNKS

    def wrap(v):
        return jnp.where(v >= SIDE, v - SIDE, v)

    def at(step, flip):
        nx, ny, nz = (wrap(v + d % SIDE) for v, d in zip((x, y, z), step))
        return (nx * SIDE + ny) * 2 + (1 - core if flip else core), nz

    loads = (
        pltpu.make_async_copy(emb_ref, raw, load_sem.at[0]),
        pltpu.make_async_copy(cluster_ref, label, load_sem.at[1]),
    )
    for load in loads:
        load.start()
    barrier = pltpu.get_barrier_semaphore()
    near_by = [at(step, 0) for step in STEPS]
    twin = at(HOME, 1)
    for spot in near_by + [twin]:
        pl.semaphore_signal(barrier, 1, device_id=spot, device_id_type=MESH)
    homes = [[
        at(tuple(-v for v in SPOTS[who][node]), 0) if node < SLOTS else
        at(tuple(-v for v in SPOTS[1 - who][SHARED[1 - who][node - SLOTS]]), 1)
        for node in range(SLOTS + len(SHARED[1 - who]))] for who in range(2)]
    for load in loads:
        load.wait()

    values = raw[...].astype(jnp.float32)
    factor = lax.rsqrt(jnp.mean(values * values, axis=1, keepdims=True) + 1e-06)
    rows[0] = (values * (factor * raw.shape[1] ** (-0.5))).astype(jnp.bfloat16)
    names[0] = jnp.broadcast_to(label[...].astype(jnp.float32), names.shape[1:])
    pl.semaphore_wait(barrier, len(STEPS) + 1)

    def remote(src, dst, send, recv, spot):
        return pltpu.make_async_remote_copy(
            src, dst, send, recv, device_id=spot, device_id_type=MESH)

    def chunk_copy(src, dst, chunk, spot):
        span = pl.ds(chunk * part, part)
        return remote(rows.at[src, span], rows.at[dst, span], row_send, row_recv.at[dst, chunk], spot)

    def name_copy(src, dst, spot):
        return remote(names.at[src], names.at[dst], name_send, name_recv.at[dst], spot)

    def pair_copy(slot, i):
        return remote(rows.at[slot], rows.at[SLOTS + i], pair_send, pair_recv.at[i], twin)

    def pair_name_copy(slot, i):
        return remote(names.at[slot], names.at[SLOTS + i], pname_send, pname_recv.at[i], twin)

    def result_copy(who, node):
        flip = int(node >= SLOTS)
        return remote(leaving.at[node], results.at[node], result_send, result_recv.at[flip],
                      homes[who][node])

    def forward(who, slot, chunk):
        for k in ORDER[who][chunk]:
            if PARENT[who][chunk][k] == slot:
                spot = near_by[WAY[who][chunk][k]]
                chunk_copy(slot, k, chunk, spot).start()
                if chunk == 0:
                    name_copy(slot, k, spot).start()

    def open_step(b):
        return jnp.broadcast_to(names[b, 0:1, :], (128, count)).T

    def pair(a, b, left, best):
        scores = lax.dot_general(rows[b], rows[a], NT, preferred_element_type=jnp.float32)
        for low in range(0, count, 128):
            tile = scores[:, low:low + 128]
            match = left == names[a, 0:1, low:low + 128]
            if a == b:
                i = lax.broadcasted_iota(jnp.int32, tile.shape, 0)
                j = lax.broadcasted_iota(jnp.int32, tile.shape, 1) + low
                match = match & (i != j)
            tile = jnp.where(match, tile, jnp.float32(-1.0))
            best = jnp.maximum(best, tile)
            if a != b:
                up = jnp.max(tile.reshape(count // 8, 8, 128), axis=0)
                held[a, :, low:low + 128] = jnp.maximum(held[a, :, low:low + 128], up)
        return best

    def close_step(b, best):
        held[b] = jnp.max(best.T.reshape(128 // 8, 8, count), axis=0)

    def program(who):
        for chunk in range(CHUNKS):
            forward(who, 0, chunk)
        for kind, one, two in TASKS[who]:
            if kind == 0:
                chunk_copy(0, one, two, twin).wait_recv()
                if two == 0:
                    name_copy(0, one, twin).wait_recv()
                forward(who, one, two)
            elif kind == 1:
                pair_copy(one, two).start()
                pair_name_copy(one, two).start()
            elif kind == 2:
                if one >= SLOTS:
                    pair_copy(0, one - SLOTS).wait_recv()
                    pair_name_copy(0, one - SLOTS).wait_recv()
                left = open_step(one)
                best = jnp.full(left.shape, -1.0, jnp.float32)
            elif kind == 3:
                best = pair(one, two, left, best)
            elif kind == 4:
                close_step(one, best)
            else:
                leaving[one] = jnp.max(held[one], axis=0, keepdims=True)
                result_copy(who, one).start()

        given, taken = len(SHARED[who]), len(SHARED[1 - who])
        own, other = results.at[1:SLOTS], results.at[SLOTS:SLOTS + given]
        remote(own, own, result_send, result_recv.at[0], twin).wait_recv()
        remote(other, other, result_send, result_recv.at[1], twin).wait_recv()
        top = jnp.max(held[0], axis=0, keepdims=True)
        for node in range(1, SLOTS + given):
            top = jnp.maximum(top, results[node])
        out_ref[...] = top

        def drain(ref, sem):
            remote(ref, ref, sem, sem, twin).wait_send()

        drain(rows.at[1:SLOTS], row_send)
        drain(names.at[1:SLOTS], name_send)
        drain(rows.at[0:given], pair_send)
        drain(names.at[0:given], pname_send)
        drain(results.at[1:SLOTS + taken], result_send)

    for who in range(2):
        pl.when(core == who)(lambda who=who: program(who))


def on_device(embeddings, cluster):
    count, width = embeddings.shape
    dma = pltpu.SemaphoreType.DMA
    best = pl.pallas_call(
        kernel,
        out_shape=jax.ShapeDtypeStruct((1, count), jnp.float32),
        in_specs=[pl.BlockSpec(memory_space=pl.ANY)] * 2,
        out_specs=pl.BlockSpec(memory_space=pltpu.VMEM),
        scratch_shapes=[
            pltpu.VMEM((count, width), jnp.bfloat16),
            pltpu.VMEM((1, count), jnp.int32),
            pltpu.VMEM((NODES, count, width), jnp.bfloat16),
            pltpu.VMEM((NODES, 8, count), jnp.float32),
            pltpu.VMEM((NODES, 8, count), jnp.float32),
            pltpu.VMEM((NODES, 1, count), jnp.float32),
            pltpu.VMEM((NODES, 1, count), jnp.float32),
            dma((2,)), dma(()), dma((SLOTS, CHUNKS)), dma(()), dma((SLOTS,)),
            dma(()), dma((TAKEN,)), dma(()), dma((TAKEN,)),
            dma(()), dma((2,)),
        ],
        compiler_params=pltpu.CompilerParams(
            collective_id=0, has_side_effects=True, vmem_limit_bytes=56 * 2**20),
    )(embeddings, cluster.reshape(1, count))
    return best.reshape(count)


def solution(mesh):
    return jax.shard_map(
        on_device,
        mesh=mesh,
        in_specs=(P(("owner", "rep"), None), P(("owner", "rep"))),
        out_specs=P(("owner", "rep")),
        check_vma=False,
    )
```

```python
import jax
import jax.numpy as jnp
from jax import lax
from jax.experimental import pallas as pl
from jax.experimental.pallas import tpu as pltpu
from jax.sharding import PartitionSpec as P

MESH = pl.DeviceIdType.MESH
SIDE = 4
HOME = (0, 0, 0)
STEPS = ((1, 0, 0), (-1, 0, 0), (0, 1, 0), (0, -1, 0), (0, 0, 1), (0, 0, -1))
SPOTS = (
    ((0, 0, 0), (1, 0, 0), (0, 1, 0), (0, 0, 1), (1, 3, 0), (2, 0, 0), (0, 1, 3), (0, 0, 2), (0, 2, 0), (3, 1, 3), (2, 3, 0), (3, 1, 2)),
    ((0, 0, 0), (3, 0, 0), (0, 0, 3), (0, 3, 0), (2, 0, 0), (0, 1, 3), (0, 3, 1), (0, 0, 2), (2, 3, 0), (1, 1, 3), (3, 0, 2), (2, 2, 0)),
)
SHARED = ((0, 1, 2, 3, 4, 5, 6, 7, 8, 9), (0, 1, 2, 3, 4, 5, 6, 7, 8))
PARENT = (
    (
        (-1, 0, 0, 0, 1, 1, 2, 3, 2, 6, 4, 9),
        (-1, 0, 0, 0, 1, 1, 2, 3, 2, 6, 4, 9),
        (-1, 0, 0, 0, 1, 1, 2, 3, 2, 6, 4, 9),
        (-1, 0, 0, 0, 1, 1, 2, 3, 2, 6, 4, 9),
    ),
    (
        (-1, 0, 0, 0, 1, 2, 3, 2, 4, 5, 7, 8),
        (-1, 0, 0, 0, 1, 2, 3, 2, 4, 5, 7, 8),
        (-1, 0, 0, 0, 1, 2, 3, 2, 4, 5, 7, 8),
        (-1, 0, 0, 0, 1, 2, 3, 2, 4, 5, 7, 8),
    ),
)
WAY = (
    (
        (-1, 0, 2, 4, 3, 0, 5, 4, 2, 1, 0, 5),
        (-1, 0, 2, 4, 3, 0, 5, 4, 2, 1, 0, 5),
        (-1, 0, 2, 4, 3, 0, 5, 4, 2, 1, 0, 5),
        (-1, 0, 2, 4, 3, 0, 5, 4, 2, 1, 0, 5),
    ),
    (
        (-1, 1, 5, 3, 1, 2, 4, 5, 3, 0, 1, 3),
        (-1, 1, 5, 3, 1, 2, 4, 5, 3, 0, 1, 3),
        (-1, 1, 5, 3, 1, 2, 4, 5, 3, 0, 1, 3),
        (-1, 1, 5, 3, 1, 2, 4, 5, 3, 0, 1, 3),
    ),
)
ORDER = (
    (
        (2, 1, 6, 3, 4, 9, 5, 7, 8, 10, 11),
        (2, 1, 6, 3, 4, 9, 5, 7, 8, 10, 11),
        (2, 1, 6, 3, 4, 9, 5, 7, 8, 10, 11),
        (2, 1, 6, 3, 4, 9, 5, 7, 8, 10, 11),
    ),
    (
        (1, 2, 4, 3, 5, 7, 8, 6, 9, 10, 11),
        (1, 2, 4, 3, 5, 7, 8, 6, 9, 10, 11),
        (1, 2, 4, 3, 5, 7, 8, 6, 9, 10, 11),
        (1, 2, 4, 3, 5, 7, 8, 6, 9, 10, 11),
    ),
)
TASKS = (
    (
        (1, 0, 0), (2, 0, 0), (3, 0, 0), (4, 0, 0), (0, 1, 0), (0, 2, 0), (0, 3, 0), (2, 12, 0), (3, 0, 12),
        (4, 12, 0), (0, 1, 1), (0, 2, 1), (0, 3, 1), (0, 1, 2), (0, 2, 2), (0, 3, 2), (0, 1, 3), (1, 1, 1),
        (2, 1, 0), (3, 0, 1), (4, 1, 0), (0, 4, 0), (0, 6, 0), (0, 2, 3), (0, 3, 3), (1, 2, 2), (1, 3, 3),
        (2, 2, 0), (3, 12, 2), (3, 0, 2), (3, 1, 2), (4, 2, 0), (2, 3, 0), (3, 0, 3), (3, 1, 3), (3, 2, 3),
        (4, 3, 0), (0, 4, 1), (2, 13, 0), (3, 1, 13), (4, 13, 0), (0, 6, 1), (2, 14, 0), (4, 14, 0),
        (0, 4, 2), (2, 15, 0), (3, 2, 15), (4, 15, 0), (0, 6, 2), (0, 4, 3), (0, 9, 0), (1, 4, 4), (2, 4, 0),
        (3, 2, 4), (3, 12, 4), (3, 14, 4), (3, 3, 4), (3, 13, 4), (4, 4, 0), (0, 5, 0), (0, 5, 1), (0, 5, 2),
        (0, 5, 3), (1, 5, 5), (2, 5, 0), (3, 2, 5), (3, 0, 5), (3, 14, 5), (3, 3, 5), (3, 15, 5), (3, 13, 5),
        (3, 4, 5), (4, 5, 0), (0, 6, 3), (0, 9, 1), (1, 6, 6), (2, 6, 0), (3, 1, 6), (3, 3, 6), (3, 13, 6),
        (3, 4, 6), (3, 5, 6), (4, 6, 0), (2, 16, 0), (4, 16, 0), (0, 7, 0), (0, 7, 1), (0, 7, 2), (0, 7, 3),
        (1, 7, 7), (0, 8, 0), (0, 8, 1), (0, 8, 2), (0, 8, 3), (1, 8, 8), (2, 7, 0), (3, 1, 7), (3, 0, 7),
        (3, 6, 7), (3, 14, 7), (3, 13, 7), (3, 16, 7), (3, 4, 7), (3, 15, 7), (3, 5, 7), (4, 7, 0), (5, 1, 0),
        (0, 9, 2), (2, 8, 0), (3, 0, 8), (3, 14, 8), (3, 13, 8), (3, 16, 8), (3, 3, 8), (3, 15, 8), (3, 5, 8),
        (3, 7, 8), (4, 8, 0), (5, 16, 0), (5, 13, 0), (5, 14, 0), (0, 9, 3), (2, 17, 0), (3, 7, 17),
        (4, 17, 0), (1, 9, 9), (2, 18, 0), (3, 6, 18), (4, 18, 0), (5, 6, 0), (2, 19, 0), (4, 19, 0),
        (2, 9, 0), (3, 2, 9), (3, 8, 9), (3, 15, 9), (3, 4, 9), (3, 5, 9), (3, 19, 9), (3, 12, 9), (3, 18, 9),
        (4, 9, 0), (5, 8, 0), (5, 2, 0), (5, 15, 0), (2, 20, 0), (3, 9, 20), (4, 20, 0), (5, 20, 0),
        (0, 10, 0), (0, 10, 1), (0, 10, 2), (0, 10, 3), (2, 10, 0), (3, 7, 10), (3, 3, 10), (3, 9, 10),
        (3, 19, 10), (3, 18, 10), (3, 17, 10), (4, 10, 0), (5, 9, 0), (5, 7, 0), (5, 19, 0), (5, 3, 0),
        (0, 11, 0), (0, 11, 1), (0, 11, 2), (0, 11, 3), (2, 11, 0), (3, 4, 11), (3, 5, 11), (3, 10, 11),
        (3, 17, 11), (3, 12, 11), (3, 18, 11), (4, 11, 0), (5, 11, 0), (5, 10, 0), (5, 4, 0), (5, 5, 0),
        (5, 17, 0), (5, 18, 0), (5, 12, 0),
    ),
    (
        (1, 0, 0), (2, 0, 0), (3, 0, 0), (4, 0, 0), (0, 1, 0), (0, 2, 0), (0, 3, 0), (2, 12, 0), (4, 12, 0),
        (0, 1, 1), (0, 2, 1), (0, 3, 1), (0, 1, 2), (0, 2, 2), (0, 3, 2), (0, 1, 3), (1, 1, 1), (2, 1, 0),
        (3, 12, 1), (3, 0, 1), (4, 1, 0), (0, 5, 0), (0, 2, 3), (0, 3, 3), (0, 4, 0), (1, 2, 2), (1, 3, 3),
        (2, 2, 0), (3, 12, 2), (3, 0, 2), (3, 1, 2), (4, 2, 0), (2, 3, 0), (3, 0, 3), (3, 1, 3), (3, 2, 3),
        (4, 3, 0), (0, 4, 1), (2, 13, 0), (3, 3, 13), (3, 2, 13), (4, 13, 0), (0, 5, 1), (0, 7, 0),
        (2, 14, 0), (3, 2, 14), (4, 14, 0), (2, 15, 0), (3, 2, 15), (4, 15, 0), (0, 4, 2), (0, 5, 2),
        (0, 7, 1), (0, 8, 0), (0, 4, 3), (1, 4, 4), (2, 4, 0), (3, 0, 4), (3, 2, 4), (3, 3, 4), (4, 4, 0),
        (0, 8, 1), (0, 5, 3), (0, 7, 2), (2, 16, 0), (3, 4, 16), (4, 16, 0), (1, 5, 5), (0, 6, 0), (0, 6, 1),
        (0, 6, 2), (0, 6, 3), (1, 6, 6), (2, 5, 0), (3, 4, 5), (3, 3, 5), (3, 12, 5), (3, 15, 5), (3, 16, 5),
        (3, 1, 5), (4, 5, 0), (0, 8, 2), (0, 7, 3), (2, 6, 0), (3, 2, 6), (3, 12, 6), (3, 16, 6), (3, 14, 6),
        (3, 1, 6), (3, 5, 6), (4, 6, 0), (1, 7, 7), (2, 17, 0), (3, 6, 17), (3, 5, 17), (4, 17, 0), (0, 8, 3),
        (2, 18, 0), (4, 18, 0), (1, 8, 8), (2, 7, 0), (3, 16, 7), (3, 0, 7), (3, 4, 7), (3, 5, 7), (3, 1, 7),
        (4, 7, 0), (5, 16, 0), (2, 19, 0), (4, 19, 0), (2, 20, 0), (4, 20, 0), (2, 8, 0), (3, 5, 8),
        (3, 1, 8), (3, 15, 8), (3, 13, 8), (3, 7, 8), (3, 19, 8), (3, 18, 8), (4, 8, 0), (5, 5, 0), (0, 9, 0),
        (0, 9, 1), (0, 9, 2), (0, 9, 3), (2, 9, 0), (3, 12, 9), (3, 15, 9), (3, 3, 9), (3, 7, 9), (3, 6, 9),
        (3, 8, 9), (3, 14, 9), (3, 19, 9), (4, 9, 0), (5, 15, 0), (5, 12, 0), (2, 21, 0), (4, 21, 0),
        (0, 10, 0), (0, 10, 1), (0, 10, 2), (0, 10, 3), (2, 10, 0), (3, 2, 10), (3, 3, 10), (3, 9, 10),
        (3, 6, 10), (3, 8, 10), (3, 14, 10), (3, 20, 10), (3, 17, 10), (3, 18, 10), (4, 10, 0), (5, 8, 0),
        (5, 9, 0), (5, 10, 0), (5, 6, 0), (5, 17, 0), (5, 20, 0), (5, 2, 0), (5, 3, 0), (5, 14, 0),
        (0, 11, 0), (0, 11, 1), (0, 11, 2), (0, 11, 3), (2, 11, 0), (3, 0, 11), (3, 1, 11), (3, 4, 11),
        (3, 7, 11), (3, 21, 11), (3, 19, 11), (3, 18, 11), (3, 13, 11), (4, 11, 0), (5, 11, 0), (5, 21, 0),
        (5, 4, 0), (5, 7, 0), (5, 18, 0), (5, 19, 0), (5, 1, 0), (5, 13, 0),
    ),
)
SLOTS = len(SPOTS[0])
TAKEN = max(len(shared) for shared in SHARED)
NODES = SLOTS + TAKEN
CHUNKS = len(PARENT[0])
NT = (((1,), (1,)), ((), ()))


def place():
    owner, z = lax.axis_index("owner"), lax.axis_index("rep")
    return owner // (2 * SIDE), (owner // 2) % SIDE, owner % 2, z


def kernel(
    emb_ref, cluster_ref, out_ref, raw, label, rows, names, held, leaving, results,
    load_sem, row_send, row_recv, name_send, name_recv, pair_send, pair_recv,
    pname_send, pname_recv, result_send, result_recv,
):
    x, y, core, z = place()
    count = raw.shape[0]
    part = count // CHUNKS

    def wrap(v):
        return jnp.where(v >= SIDE, v - SIDE, v)

    def at(step, flip):
        nx, ny, nz = (wrap(v + d % SIDE) for v, d in zip((x, y, z), step))
        return (nx * SIDE + ny) * 2 + (1 - core if flip else core), nz

    loads = (
        pltpu.make_async_copy(emb_ref, raw, load_sem.at[0]),
        pltpu.make_async_copy(cluster_ref, label, load_sem.at[1]),
    )
    for load in loads:
        load.start()
    barrier = pltpu.get_barrier_semaphore()
    near_by = [at(step, 0) for step in STEPS]
    twin = at(HOME, 1)
    for spot in near_by + [twin]:
        pl.semaphore_signal(barrier, 1, device_id=spot, device_id_type=MESH)
    homes = [[
        at(tuple(-v for v in SPOTS[who][node]), 0) if node < SLOTS else
        at(tuple(-v for v in SPOTS[1 - who][SHARED[1 - who][node - SLOTS]]), 1)
        for node in range(SLOTS + len(SHARED[1 - who]))] for who in range(2)]
    for load in loads:
        load.wait()

    values = raw[...].astype(jnp.float32)
    factor = lax.rsqrt(jnp.mean(values * values, axis=1, keepdims=True) + 1e-06)
    rows[0] = (values * (factor * raw.shape[1] ** (-0.5))).astype(jnp.bfloat16)
    names[0] = label[...].astype(jnp.float32)
    pl.semaphore_wait(barrier, len(STEPS) + 1)

    def remote(src, dst, send, recv, spot):
        return pltpu.make_async_remote_copy(
            src, dst, send, recv, device_id=spot, device_id_type=MESH)

    def chunk_copy(src, dst, chunk, spot):
        span = pl.ds(chunk * part, part)
        return remote(rows.at[src, span], rows.at[dst, span], row_send, row_recv.at[dst, chunk], spot)

    def name_copy(src, dst, spot):
        return remote(names.at[src], names.at[dst], name_send, name_recv.at[dst], spot)

    def pair_copy(slot, i):
        return remote(rows.at[slot], rows.at[SLOTS + i], pair_send, pair_recv.at[i], twin)

    def pair_name_copy(slot, i):
        return remote(names.at[slot], names.at[SLOTS + i], pname_send, pname_recv.at[i], twin)

    def result_copy(who, node):
        flip = int(node >= SLOTS)
        return remote(leaving.at[node], results.at[node], result_send, result_recv.at[flip],
                      homes[who][node])

    def forward(who, slot, chunk):
        for k in ORDER[who][chunk]:
            if PARENT[who][chunk][k] == slot:
                spot = near_by[WAY[who][chunk][k]]
                chunk_copy(slot, k, chunk, spot).start()
                if chunk == 0:
                    name_copy(slot, k, spot).start()

    def open_step(b):
        return jnp.broadcast_to(names[b, 0:1, :], (128, count)).T

    def pair(a, b, left, best):
        scores = lax.dot_general(rows[b], rows[a], NT, preferred_element_type=jnp.float32)
        for low in range(0, count, 128):
            tile = scores[:, low:low + 128]
            match = left == names[a, 0:1, low:low + 128]
            if a == b:
                i = lax.broadcasted_iota(jnp.int32, tile.shape, 0)
                j = lax.broadcasted_iota(jnp.int32, tile.shape, 1) + low
                match = match & (i != j)
            tile = jnp.where(match, tile, jnp.float32(-1.0))
            best = jnp.maximum(best, tile)
            if a != b:
                up = jnp.max(tile.reshape(count // 8, 8, 128), axis=0)
                held[a, :, low:low + 128] = jnp.maximum(held[a, :, low:low + 128], up)
        return best

    def close_step(b, best):
        held[b] = jnp.max(best.T.reshape(128 // 8, 8, count), axis=0)

    def program(who):
        for chunk in range(CHUNKS):
            forward(who, 0, chunk)
        for kind, one, two in TASKS[who]:
            if kind == 0:
                chunk_copy(0, one, two, twin).wait_recv()
                if two == 0:
                    name_copy(0, one, twin).wait_recv()
                forward(who, one, two)
            elif kind == 1:
                pair_copy(one, two).start()
                pair_name_copy(one, two).start()
            elif kind == 2:
                if one >= SLOTS:
                    pair_copy(0, one - SLOTS).wait_recv()
                    pair_name_copy(0, one - SLOTS).wait_recv()
                left = open_step(one)
                best = jnp.full(left.shape, -1.0, jnp.float32)
            elif kind == 3:
                best = pair(one, two, left, best)
            elif kind == 4:
                close_step(one, best)
            else:
                leaving[one] = jnp.max(held[one], axis=0, keepdims=True)
                result_copy(who, one).start()

        given, taken = len(SHARED[who]), len(SHARED[1 - who])
        own, other = results.at[1:SLOTS], results.at[SLOTS:SLOTS + given]
        remote(own, own, result_send, result_recv.at[0], twin).wait_recv()
        remote(other, other, result_send, result_recv.at[1], twin).wait_recv()
        top = jnp.max(held[0], axis=0, keepdims=True)
        for node in range(1, SLOTS + given):
            top = jnp.maximum(top, results[node])
        out_ref[...] = top

        def drain(ref, sem):
            remote(ref, ref, sem, sem, twin).wait_send()

        drain(rows.at[1:SLOTS], row_send)
        drain(names.at[1:SLOTS], name_send)
        drain(rows.at[0:given], pair_send)
        drain(names.at[0:given], pname_send)
        drain(results.at[1:SLOTS + taken], result_send)

    for who in range(2):
        pl.when(core == who)(lambda who=who: program(who))


def on_device(embeddings, cluster):
    count, width = embeddings.shape
    dma = pltpu.SemaphoreType.DMA
    best = pl.pallas_call(
        kernel,
        out_shape=jax.ShapeDtypeStruct((1, count), jnp.float32),
        in_specs=[pl.BlockSpec(memory_space=pl.ANY)] * 2,
        out_specs=pl.BlockSpec(memory_space=pltpu.VMEM),
        scratch_shapes=[
            pltpu.VMEM((count, width), jnp.bfloat16),
            pltpu.VMEM((1, count), jnp.int32),
            pltpu.VMEM((NODES, count, width), jnp.bfloat16),
            pltpu.VMEM((NODES, 1, count), jnp.float32),
            pltpu.VMEM((NODES, 8, count), jnp.float32),
            pltpu.VMEM((NODES, 1, count), jnp.float32),
            pltpu.VMEM((NODES, 1, count), jnp.float32),
            dma((2,)), dma(()), dma((SLOTS, CHUNKS)), dma(()), dma((SLOTS,)),
            dma(()), dma((TAKEN,)), dma(()), dma((TAKEN,)),
            dma(()), dma((2,)),
        ],
        compiler_params=pltpu.CompilerParams(
            collective_id=0, has_side_effects=True, vmem_limit_bytes=56 * 2**20),
    )(embeddings, cluster.reshape(1, count))
    return best.reshape(count)


def solution(mesh):
    return jax.shard_map(
        on_device,
        mesh=mesh,
        in_specs=(P(("owner", "rep"), None), P(("owner", "rep"))),
        out_specs=P(("owner", "rep")),
        check_vma=False,
    )
```
